256 devices in a mesh: blk: 64 (over x, y, z_hi, core), grp: 4 (over z_lo).
Axes of the slice: x: 4, y: 4, z: 8 (z_hi: 2, z_lo: 4; z = z_hi * 4 + z_lo), core: 2. Of those that a mesh axis runs over, the one named last changes fastest.
Arguments:
- generated: bfloat16 [40960, 2048], P('blk', 'grp'), may hold values from -6 to 6
- reference_set: bfloat16 [40960, 2048], P('blk', 'grp'), may hold values from -6 to 6
- partners: int32 [2, 64], replicated, may hold values from 0 to 63, as said below
Outputs:
- proof: float32 [40960], P('blk')
- feature_grads: float32 [40960, 2048], P('blk', 'grp')
The draws below stay inside these ranges and needn't reach their ends.
Inputs may be any that keep to these rules, and one draw needn't show every extreme that they name: In each round every block's partner is its own index with one fixed nonzero set of bits flipped, the same set for all blocks of that round; the sets of the 2 rounds differ, so partners pair up and no block meets the same partner twice.
All inputs are finite; a program needn't handle non-finite values.
Results may differ from the reference program's by a relative error of at most 0.0026.
Values may be sent and summed in bfloat16 or wider, within the bound.
No kernel may reach another device: no remote copies, remote signals or barrier semaphores. Data moves between devices by JAX's collectives and lax.ppermute only.
A program may use at most 64 MiB of HBM per device.

```python
import jax
import jax.numpy as jnp
from jax import lax

F = 2048
ROWS = 640
ROUNDS = 2
TOTAL = 40960
N_BLK = 64


def draw_partners(key, part):
    key = jax.random.fold_in(key, 11)
    flip_masks = (jax.random.permutation(key, N_BLK - 1)[:ROUNDS] + 1).astype(jnp.int32)
    blocks = jnp.arange(N_BLK, dtype=jnp.int32)
    return jnp.bitwise_xor(blocks[None, :], flip_masks[:, None]).astype(jnp.int32)


def level_of(stream_key, dims, shards, least, high):
    factor_of = 1.0
    for dim, parts in shards:
        draws = jax.random.uniform(jax.random.fold_in(jax.random.fold_in(stream_key, 6), dim), (parts,), jnp.float32, least / len(shards), high / len(shards))
        factor_of = factor_of * jnp.repeat(jnp.exp(draws), dims[dim] // parts).reshape((-1,) + (1,) * (len(dims) - 1 - dim))
    return factor_of


def scatter_about(key, extent, scale, reach, shards=(), kind=jnp.bfloat16):
    drawn = jax.random.normal(key, extent, jnp.float32) * scale
    if len(shards) > 0:
        drawn = level_of(key, extent, shards, -0.22, 0.18) * drawn
    return jnp.clip(drawn, min=-reach, max=reach).astype(kind)


def setup_inputs(seed: int = 0) -> dict:
    streams_of = jax.random.split(jax.random.key(seed), 4)
    generated = scatter_about(streams_of[0], (TOTAL, F), 1.2, 6.0, ((0, 64), (1, 4)))
    reference_set = scatter_about(streams_of[1], (TOTAL, F), 1.0, 6.0, ((0, 64), (1, 4)))
    partners = draw_partners(jax.random.fold_in(streams_of[3], 71), 0)
    return dict(generated=generated, reference_set=reference_set, partners=partners)


def cross_gram(left, right):
    return lax.dot_general(left, right, (((1,), (1,)), ((), ())), preferred_element_type=jnp.float32)


def reference(generated, reference_set, partners):
    gen_blocks = generated.reshape(N_BLK, ROWS, F)
    ref_blocks = reference_set.reshape(N_BLK, ROWS, F)
    wit_scale = (F / (ROUNDS * ROWS)) ** 0.5
    grad_scale = 1.0 / (ROUNDS * ROWS) ** 0.5
    proof = jnp.zeros((N_BLK, ROWS), jnp.float32)
    grads = jnp.zeros((N_BLK, ROWS, F), jnp.float32)
    for round_index in range(ROUNDS):
        def one_block(block_index):
            partner_id = partners[round_index, block_index]
            own_rows = gen_blocks[block_index]
            partner_gen = gen_blocks[partner_id]
            partner_ref = ref_blocks[partner_id]
            gram_same = cross_gram(own_rows, partner_gen) / F
            gram_cross = cross_gram(own_rows, partner_ref) / F
            kernel_diff = jnp.sum((gram_same + 1.0) ** 3 - (gram_cross + 1.0) ** 3, axis=1)
            weight_same = (3.0 * (gram_same + 1.0) ** 2).astype(jnp.bfloat16)
            weight_cross = (3.0 * (gram_cross + 1.0) ** 2).astype(jnp.bfloat16)
            grad_terms = jnp.dot(weight_same, partner_gen, preferred_element_type=jnp.float32) - jnp.dot(weight_cross, partner_ref, preferred_element_type=jnp.float32)
            return kernel_diff, grad_terms
        kernel_diff, grad_terms = lax.map(one_block, jnp.arange(N_BLK, dtype=jnp.int32))
        proof = proof + wit_scale * kernel_diff
        grads = grads + grad_scale * grad_terms
    return proof.reshape(TOTAL), grads.reshape(TOTAL, F)
```

```python
import jax
import jax.numpy as jnp
from jax import lax
from jax.experimental import pallas as pl
from jax.experimental.pallas import tpu as pltpu
from jax.sharding import PartitionSpec as P

TILE = 128


def grp_swap(value, distance):
    size = lax.axis_size("grp")
    return lax.ppermute(value, "grp", [(k, k ^ distance) for k in range(size)])


def blk_swap(value, mask, mirror_bit):
    blocks, groups = lax.axis_size("blk"), lax.axis_size("grp")
    if mask & mirror_bit:
        pairs = [
            (b * groups + k, (b ^ mask) * groups + groups - 1 - k)
            for b in range(blocks)
            for k in range(groups)
        ]
        return lax.ppermute(value, ("blk", "grp"), pairs)
    return lax.ppermute(value, "blk", [(b, b ^ mask) for b in range(blocks)])


def exchange(value, mask, mirror_bit):
    def branch(fixed):
        return lambda v: blk_swap(v, fixed, mirror_bit)

    masks = range(1, lax.axis_size("blk"))
    return lax.switch(mask - 1, [branch(m) for m in masks], value)


def tile_kernel(full_width, grad_scale, wit_scale, flips, *refs):
    slots = len(refs) // 2 - 1
    left = refs[:slots]
    rows_of = refs[slots : slots + 2]
    proof = refs[slots + 2]
    grads = refs[slots + 3 :]
    total = [jnp.zeros(g.shape, jnp.float32) for g in grads]
    witness = jnp.zeros(proof.shape, jnp.float32)
    for index, rows in enumerate(rows_of):
        flip = flips[index]
        count = rows.shape[1]
        gram = jnp.zeros((TILE, count), jnp.float32)
        for slot in range(slots):
            gram += lax.dot_general(
                left[slot][...],
                rows[slot ^ flip],
                (((1,), (1,)), ((), ())),
                preferred_element_type=jnp.float32,
            )
        column = lax.broadcasted_iota(jnp.int32, gram.shape, 1)
        sign = jnp.where(column < count // 2, 1.0, -1.0)
        shifted = gram * (1.0 / full_width) + 1.0
        squared = shifted * shifted
        signed = squared * sign
        witness += jnp.sum(signed * shifted, axis=1, keepdims=True)
        weight = (3.0 * signed).astype(jnp.bfloat16)
        for slot in range(slots):
            total[slot] += jnp.dot(
                weight, rows[slot ^ flip], preferred_element_type=jnp.float32
            )
    proof[...] = witness * wit_scale
    for slot in range(slots):
        grads[slot][...] = (total[slot] * grad_scale).astype(grads[slot].dtype)


def on_device(generated, reference_set, partners):
    block_rows, feat_width = generated.shape
    groups = lax.axis_size("grp")
    full_width = feat_width * groups
    rounds_count = partners.shape[0]
    share = block_rows // groups
    mirror_bit = 2
    wit_scale = (full_width / (rounds_count * block_rows)) ** 0.5
    grad_scale = 1.0 / (rounds_count * block_rows) ** 0.5
    here = lax.axis_index("grp")

    both = jnp.stack(
        [
            generated.reshape(groups, share, feat_width),
            reference_set.reshape(groups, share, feat_width),
        ],
        axis=1,
    )
    pieces = [lax.dynamic_index_in_dim(both, here, 0, False)]
    for distance in range(1, groups):
        piece = lax.dynamic_index_in_dim(both, here ^ distance, 0, False)
        pieces.append(grp_swap(piece, distance))
    own_rows = jnp.stack(pieces).reshape(groups, 2 * share, feat_width)
    left = [generated] + [grp_swap(generated, d) for d in range(1, groups)]

    masks = partners[:, 0]
    met = [exchange(own_rows, masks[r], mirror_bit) for r in range(rounds_count)]
    flips = jnp.where(masks & mirror_bit > 0, groups - 1, 0).astype(jnp.int32)

    tile = pl.BlockSpec((TILE, feat_width), lambda i: (i, 0))
    whole = pl.BlockSpec((groups, 2 * share, feat_width), lambda i: (0, 0, 0))
    out = pl.pallas_call(
        lambda *refs: tile_kernel(full_width, grad_scale, wit_scale, *refs),
        grid=(block_rows // TILE,),
        in_specs=[pl.BlockSpec(memory_space=pltpu.SMEM)]
        + [tile] * groups
        + [whole] * rounds_count,
        out_specs=[pl.BlockSpec((TILE, 1), lambda i: (i, 0))] + [tile] * groups,
        out_shape=[jax.ShapeDtypeStruct((block_rows, 1), jnp.float32)]
        + [
            jax.ShapeDtypeStruct(
                (block_rows, feat_width), jnp.bfloat16 if d else jnp.float32
            )
            for d in range(groups)
        ],
        compiler_params=pltpu.CompilerParams(vmem_limit_bytes=40 * 2**20),
    )(flips, *left, *met)
    proof = lax.psum(out[0].reshape(block_rows), "grp")
    grads = out[1]
    for distance in range(1, groups):
        grads = grads + grp_swap(out[1 + distance], distance).astype(jnp.float32)
    return (proof, grads)


def solution(mesh):
    return jax.shard_map(
        on_device,
        mesh=mesh,
        in_specs=(P("blk", "grp"), P("blk", "grp"), P()),
        out_specs=(P("blk"), P("blk", "grp")),
        check_vma=False,
    )
```

```python
import jax
import jax.numpy as jnp
from jax import lax
from jax.experimental import pallas as pl
from jax.experimental.pallas import tpu as pltpu
from jax.sharding import PartitionSpec as P

TILE = 128
CORE, FAR = 1, 2


def grp_swap(value, distance):
    size = lax.axis_size("grp")
    return lax.ppermute(value, "grp", [(k, k ^ distance) for k in range(size)])


def blk_swap(value, mask):
    blocks = lax.axis_size("blk")
    return lax.ppermute(value, "blk", [(b, b ^ mask) for b in range(blocks)])


def far_swap(value):
    blocks, groups = lax.axis_size("blk"), lax.axis_size("grp")
    pairs = [
        (b * groups + k, (b ^ FAR) * groups + groups - 1 - k)
        for b in range(blocks)
        for k in range(groups)
    ]
    return lax.ppermute(value, ("blk", "grp"), pairs)


def plane_hop(value, step):
    stride = 2 * FAR
    masks = range(stride, lax.axis_size("blk"), stride)
    branches = [lambda v, m=m: blk_swap(v, m) for m in masks]
    return lax.switch(step, [lambda v: v] + branches, value)


def tile_kernel(full_width, grad_scale, wit_scale, first, *refs):
    slots = len(refs) // 2 - 1
    left = refs[:slots]
    met, proof, *grads = refs[slots:]
    total = [jnp.zeros(g.shape, jnp.float32) for g in grads]
    witness = jnp.zeros(proof.shape, jnp.float32)
    for index in range(met.shape[0]):
        count = met.shape[2]
        gram = jnp.zeros((TILE, count), jnp.float32)
        for slot in range(slots):
            gram += lax.dot_general(
                left[slot][...],
                met[index, slot ^ first[0]],
                (((1,), (1,)), ((), ())),
                preferred_element_type=jnp.float32,
            )
        column = lax.broadcasted_iota(jnp.int32, gram.shape, 1)
        sign = jnp.where(column < count // 2, 1.0, -1.0)
        shifted = gram * (1.0 / full_width) + 1.0
        squared = shifted * shifted
        signed = squared * sign
        witness += jnp.sum(signed * shifted, axis=1, keepdims=True)
        weight = (3.0 * signed).astype(jnp.bfloat16)
        for slot in range(slots):
            total[slot] += jnp.dot(
                weight, met[index, slot ^ first[0]], preferred_element_type=jnp.float32
            )
    proof[...] = witness * wit_scale
    for slot in range(slots):
        grads[slot][...] = (total[slot] * grad_scale).astype(grads[slot].dtype)


def on_device(generated, reference_set, partners):
    block_rows, feat_width = generated.shape
    groups = lax.axis_size("grp")
    full_width = feat_width * groups
    rounds_count = partners.shape[0]
    share = block_rows // groups
    wit_scale = (full_width / (rounds_count * block_rows)) ** 0.5
    grad_scale = 1.0 / (rounds_count * block_rows) ** 0.5
    here = lax.axis_index("grp")

    both = jnp.concatenate(
        [
            generated.reshape(groups, share, feat_width),
            reference_set.reshape(groups, share, feat_width),
        ],
        axis=1,
    )
    own_rows = lax.all_to_all(both, "grp", 0, 0)
    own_rows, generated = lax.optimization_barrier((own_rows, generated))
    left = [generated] + [grp_swap(generated, d) for d in range(1, groups)]

    masks = partners[:, 0]
    any_far = jnp.any(masks & FAR > 0)
    far_rows = lax.cond(any_far, far_swap, lambda v: v, own_rows)

    def meet(carry, mask):
        rows = jnp.where(mask & FAR > 0, far_rows, own_rows)
        rows = lax.cond(mask & CORE > 0, lambda v: blk_swap(v, CORE), lambda v: v, rows)
        return carry, plane_hop(rows, mask // (2 * FAR))

    _, met = lax.scan(meet, 0, masks)
    first = here.astype(jnp.int32).reshape(1)

    tile = pl.BlockSpec((TILE, feat_width), lambda i: (i, 0))
    whole = pl.BlockSpec(met.shape, lambda i: (0, 0, 0, 0))
    out = pl.pallas_call(
        lambda *refs: tile_kernel(full_width, grad_scale, wit_scale, *refs),
        grid=(block_rows // TILE,),
        in_specs=[pl.BlockSpec(memory_space=pltpu.SMEM)]
        + [tile] * groups
        + [whole],
        out_specs=[pl.BlockSpec((TILE, 1), lambda i: (i, 0))] + [tile] * groups,
        out_shape=[jax.ShapeDtypeStruct((block_rows, 1), jnp.float32)]
        + [
            jax.ShapeDtypeStruct(
                (block_rows, feat_width), jnp.bfloat16 if d else jnp.float32
            )
            for d in range(groups)
        ],
        compiler_params=pltpu.CompilerParams(vmem_limit_bytes=40 * 2**20),
    )(first, *left, met)
    proof = out[0].reshape(block_rows)
    for distance in (1, 2):
        proof = proof + grp_swap(proof, distance)
    grads = out[1]
    for distance in range(1, groups):
        grads = grads + grp_swap(out[1 + distance], distance).astype(jnp.float32)
    return (proof, grads)


def solution(mesh):
    return jax.shard_map(
        on_device,
        mesh=mesh,
        in_specs=(P("blk", "grp"), P("blk", "grp"), P()),
        out_specs=(P("blk"), P("blk", "grp")),
        check_vma=False,
    )
```

```python
import jax
import jax.numpy as jnp
from jax import lax
from jax.experimental import pallas as pl
from jax.experimental.pallas import tpu as pltpu
from jax.sharding import PartitionSpec as P

TILE = 320
CORE, FAR = 1, 2


def grp_swap(value, distance):
    size = lax.axis_size("grp")
    return lax.ppermute(value, "grp", [(k, k ^ distance) for k in range(size)])


def blk_swap(value, mask):
    blocks = lax.axis_size("blk")
    return lax.ppermute(value, "blk", [(b, b ^ mask) for b in range(blocks)])


def far_swap(value):
    blocks, groups = lax.axis_size("blk"), lax.axis_size("grp")
    pairs = [
        (b * groups + k, (b ^ FAR) * groups + groups - 1 - k)
        for b in range(blocks)
        for k in range(groups)
    ]
    return lax.ppermute(value, ("blk", "grp"), pairs)


def plane_hop(value, step):
    stride = 2 * FAR
    masks = range(stride, lax.axis_size("blk"), stride)
    branches = [lambda v, m=m: blk_swap(v, m) for m in masks]
    return lax.switch(step, [lambda v: v] + branches, value)


def tile_kernel(full_width, grad_scale, wit_scale, chunk, first, *refs):
    slots = (len(refs) - 2) // 2
    left = refs[:slots]
    met, proof, *grads = refs[slots:]
    right = [met.at[slot ^ first[0]] for slot in range(slots)]
    gram = jnp.zeros((TILE, met.shape[1]), jnp.float32)
    for slot in range(slots):
        gram += lax.dot_general(
            left[slot][...],
            right[slot][...],
            (((1,), (1,)), ((), ())),
            preferred_element_type=jnp.float32,
        )
    column = lax.broadcasted_iota(jnp.int32, gram.shape, 1)
    sign = jnp.where(column // chunk % 2 == 0, 1.0, -1.0)
    shifted = gram * (1.0 / full_width) + 1.0
    signed = shifted * shifted * sign
    proof[...] = jnp.sum(signed * shifted, axis=1, keepdims=True) * wit_scale
    weight = (3.0 * signed).astype(jnp.bfloat16)
    for slot in range(slots):
        part = jnp.dot(weight, right[slot][...], preferred_element_type=jnp.float32)
        grads[slot][...] = (part * grad_scale).astype(grads[slot].dtype)


def on_device(generated, reference_set, partners):
    block_rows, feat_width = generated.shape
    groups = lax.axis_size("grp")
    full_width = feat_width * groups
    rounds_count = partners.shape[0]
    share = block_rows // groups
    wit_scale = (full_width / (rounds_count * block_rows)) ** 0.5
    grad_scale = 1.0 / (rounds_count * block_rows) ** 0.5
    here = lax.axis_index("grp")

    both = jnp.concatenate(
        [
            generated.reshape(groups, share, feat_width),
            reference_set.reshape(groups, share, feat_width),
        ],
        axis=1,
    )
    own_rows = lax.all_to_all(both, "grp", 0, 0)
    own_rows, generated = lax.optimization_barrier((own_rows, generated))
    far_rows = far_swap(own_rows)
    left = [generated] + [grp_swap(generated, d) for d in range(1, groups)]

    masks = partners[:, 0]
    far_bits = masks // FAR % 2
    order = jnp.where(far_bits[0] > far_bits[1], 1, 0)
    near_count = rounds_count - jnp.sum(far_bits)

    def meet(rows):
        def body(index, met):
            mask = masks[index ^ order]
            sent = lax.cond(
                mask % 2 == CORE, lambda v: blk_swap(v, CORE), lambda v: v, rows
            )
            got = plane_hop(sent, mask // (2 * FAR))
            return lax.dynamic_update_slice(met, got, (0, index * 2 * share, 0))

        return body

    met = jnp.zeros((groups, rounds_count * 2 * share, feat_width), generated.dtype)
    met = lax.fori_loop(0, near_count, meet(own_rows), met)
    met = lax.fori_loop(near_count, rounds_count, meet(far_rows), met)
    first = here.astype(jnp.int32).reshape(1)

    tile = pl.BlockSpec((TILE, feat_width), lambda i: (i, 0))
    out = pl.pallas_call(
        lambda *refs: tile_kernel(full_width, grad_scale, wit_scale, share, *refs),
        grid=(block_rows // TILE,),
        in_specs=[pl.BlockSpec(memory_space=pltpu.SMEM)]
        + [tile] * groups
        + [pl.BlockSpec(met.shape, lambda i: (0, 0, 0))],
        out_specs=[pl.BlockSpec((TILE, 1), lambda i: (i, 0))] + [tile] * groups,
        out_shape=[jax.ShapeDtypeStruct((block_rows, 1), jnp.float32)]
        + [
            jax.ShapeDtypeStruct(
                (block_rows, feat_width), jnp.bfloat16 if d % 2 else jnp.float32
            )
            for d in range(groups)
        ],
        compiler_params=pltpu.CompilerParams(vmem_limit_bytes=40 * 2**20),
    )(first, *left, met)
    mine, near_part, across, across_part = out[1:]
    across = across + grp_swap(across_part, 1).astype(jnp.float32)
    near_part = grp_swap(near_part, 1).astype(jnp.float32)
    across = grp_swap(across.astype(jnp.bfloat16), 2).astype(jnp.float32)
    grads = mine + near_part + across
    proofs = jnp.broadcast_to(out[0].reshape(1, block_rows), (groups, block_rows))
    proof = jnp.sum(lax.all_to_all(proofs, "grp", 0, 0), axis=0)
    return (proof, grads)


def solution(mesh):
    return jax.shard_map(
        on_device,
        mesh=mesh,
        in_specs=(P("blk", "grp"), P("blk", "grp"), P()),
        out_specs=(P("blk"), P("blk", "grp")),
        check_vma=False,
    )
```

```python
import jax
import jax.numpy as jnp
from jax import lax
from jax.experimental import pallas as pl
from jax.experimental.pallas import tpu as pltpu
from jax.sharding import PartitionSpec as P

TILE = 320
CORE, FAR = 1, 2


def grp_swap(value, distance):
    size = lax.axis_size("grp")
    return lax.ppermute(value, "grp", [(k, k ^ distance) for k in range(size)])


def blk_swap(value, mask):
    blocks = lax.axis_size("blk")
    return lax.ppermute(value, "blk", [(b, b ^ mask) for b in range(blocks)])


def far_swap(value):
    blocks, groups = lax.axis_size("blk"), lax.axis_size("grp")
    pairs = [
        (b * groups + k, (b ^ FAR) * groups + groups - 1 - k)
        for b in range(blocks)
        for k in range(groups)
    ]
    return lax.ppermute(value, ("blk", "grp"), pairs)


def plane_hop(value, step):
    stride = 2 * FAR
    masks = range(stride, lax.axis_size("blk"), stride)
    branches = [lambda v, m=m: blk_swap(v, m) for m in masks]
    return lax.switch(step, [lambda v: v] + branches, value)


def weight_kernel(full_width, grad_scale, wit_scale, chunk, first, *refs):
    slots = len(refs) - 4
    left, (met, proof, weight, part) = refs[:slots], refs[slots:]
    gram = jnp.zeros(weight.shape, jnp.float32)
    for slot in range(slots):
        gram += lax.dot_general(
            left[slot][...],
            met[slot ^ first[0]],
            (((1,), (1,)), ((), ())),
            preferred_element_type=jnp.float32,
        )
    column = lax.broadcasted_iota(jnp.int32, gram.shape, 1)
    sign = jnp.where((column // chunk) % 2 == 0, 1.0, -1.0)
    shifted = gram * (1.0 / full_width) + 1.0
    signed = shifted * shifted * sign
    proof[...] = jnp.sum(signed * shifted, axis=1, keepdims=True) * wit_scale
    weight[...] = (3.0 * signed).astype(jnp.bfloat16)
    gradient_part(grad_scale, weight[...], met, slots - 1 ^ first[0], part)


def gradient_part(grad_scale, weight, met, slot, out):
    part = jnp.dot(weight, met[slot], preferred_element_type=jnp.float32)
    out[...] = (part * grad_scale).astype(out.dtype)


def rest_kernel(grad_scale, first, weight, met, *outs):
    for slot, out in enumerate(outs):
        gradient_part(grad_scale, weight[...], met, slot ^ first[0], out)


def untouched(shape, dtype):
    return pl.pallas_call(
        lambda out: None,
        out_specs=pl.BlockSpec(memory_space=pl.ANY),
        out_shape=jax.ShapeDtypeStruct(shape, dtype),
    )()


def on_device(generated, reference_set, partners):
    block_rows, feat_width = generated.shape
    groups = lax.axis_size("grp")
    full_width = feat_width * groups
    rounds_count = partners.shape[0]
    share = block_rows // groups
    wit_scale = (full_width / (rounds_count * block_rows)) ** 0.5
    grad_scale = 1.0 / (rounds_count * block_rows) ** 0.5
    here = lax.axis_index("grp")

    both = jnp.concatenate(
        [
            generated.reshape(groups, share, feat_width),
            reference_set.reshape(groups, share, feat_width),
        ],
        axis=1,
    )
    masks = [partners[r, 0] for r in range(rounds_count)]
    far_bits = [(m >> 1) & 1 for m in masks]
    swapped = far_bits[0] > far_bits[1]
    masks = [
        jnp.where(swapped, masks[1], masks[0]),
        jnp.where(swapped, masks[0], masks[1]),
    ]
    near_count = rounds_count - far_bits[0] - far_bits[1]
    met = untouched((groups, rounds_count * 2 * share, feat_width), generated.dtype)
    first = here.astype(jnp.int32).reshape(1)
    own_rows = lax.all_to_all(both, "grp", 0, 0)
    own_rows, generated = lax.optimization_barrier((own_rows, generated))
    far_rows = far_swap(own_rows)
    left = [generated] + [grp_swap(generated, d) for d in range(1, groups)]

    def put(met, got, index):
        return lax.dynamic_update_slice(met, got, (0, index * 2 * share, 0))

    def meet(rows):
        def body(index, carry):
            met, mask, later = carry
            got = plane_hop(rows, mask >> 2)
            met = lax.cond(
                (mask & CORE) > 0,
                lambda m, g, i: put(m, blk_swap(g, CORE), i),
                put,
                met,
                got,
                index,
            )
            return met, later, later

        return body

    carry = (met, *masks)
    carry = lax.fori_loop(0, near_count, meet(own_rows), carry)
    met, _, _ = lax.fori_loop(near_count, rounds_count, meet(far_rows), carry)

    def tiled(width):
        return pl.BlockSpec((TILE, width), lambda i: (i, 0))

    def shaped(width, dtype):
        return jax.ShapeDtypeStruct((block_rows, width), dtype)

    scalar = pl.BlockSpec(memory_space=pltpu.SMEM)
    whole = pl.BlockSpec(met.shape, lambda i: (0, 0, 0))
    params = pltpu.CompilerParams(vmem_limit_bytes=40 * 2**20)
    columns = met.shape[1]
    proof, weight, across_part = pl.pallas_call(
        lambda *refs: weight_kernel(full_width, grad_scale, wit_scale, share, *refs),
        grid=(block_rows // TILE,),
        in_specs=[scalar] + [tiled(feat_width)] * groups + [whole],
        out_specs=[tiled(1), tiled(columns), tiled(feat_width)],
        out_shape=[
            shaped(1, jnp.float32),
            shaped(columns, jnp.bfloat16),
            shaped(feat_width, jnp.bfloat16),
        ],
        compiler_params=params,
    )(first, *left, met)
    cut = block_rows * 2 // 5
    spans = (slice(0, cut), slice(cut, block_rows))
    halves = [grp_swap(across_part[span], 1) for span in spans]
    mine, near_part, across = pl.pallas_call(
        lambda *refs: rest_kernel(grad_scale, *refs),
        grid=(block_rows // TILE,),
        in_specs=[scalar, tiled(columns), whole],
        out_specs=[tiled(feat_width)] * 3,
        out_shape=[
            shaped(feat_width, jnp.float32),
            shaped(feat_width, jnp.bfloat16),
            shaped(feat_width, jnp.float32),
        ],
        compiler_params=params,
    )(first, weight, met)
    crossed = []
    for span, got in zip(spans, halves):
        total = across[span] + got.astype(jnp.float32)
        crossed.append(grp_swap(total.astype(jnp.bfloat16), 2))
    near_part = grp_swap(near_part, 1).astype(jnp.float32)
    across = jnp.concatenate(crossed).astype(jnp.float32)
    grads = mine + near_part + across
    proofs = jnp.broadcast_to(proof.reshape(1, block_rows), (groups, block_rows))
    proof = jnp.sum(lax.all_to_all(proofs, "grp", 0, 0), axis=0)
    return (proof, grads)


def solution(mesh):
    return jax.shard_map(
        on_device,
        mesh=mesh,
        in_specs=(P("blk", "grp"), P("blk", "grp"), P()),
        out_specs=(P("blk"), P("blk", "grp")),
        check_vma=False,
    )
```

```python
import jax
import jax.numpy as jnp
from jax import lax
from jax.experimental import pallas as pl
from jax.experimental.pallas import tpu as pltpu
from jax.sharding import PartitionSpec as P

TILE = 320
CORE, FAR = 1, 2


def grp_swap(value, distance):
    size = lax.axis_size("grp")
    return lax.ppermute(value, "grp", [(k, k ^ distance) for k in range(size)])


def blk_swap(value, mask):
    blocks = lax.axis_size("blk")
    return lax.ppermute(value, "blk", [(b, b ^ mask) for b in range(blocks)])


def far_swap(value):
    blocks, groups = lax.axis_size("blk"), lax.axis_size("grp")
    pairs = [
        (b * groups + k, (b ^ FAR) * groups + groups - 1 - k)
        for b in range(blocks)
        for k in range(groups)
    ]
    return lax.ppermute(value, ("blk", "grp"), pairs)


def plane_hop(value, step):
    stride = 2 * FAR
    masks = range(stride, lax.axis_size("blk"), stride)
    branches = [lambda v, m=m: blk_swap(v, m) for m in masks]
    return lax.switch(step, [lambda v: v] + branches, value)


def weight_kernel(full_width, grad_scale, wit_scale, chunk, *refs):
    slots = len(refs) - 5
    left, (met, proof, weight, *parts) = refs[:slots], refs[slots:]
    gram = jnp.zeros(weight.shape, jnp.float32)
    for slot in range(slots):
        gram += lax.dot_general(
            left[slot][...],
            met[slot],
            (((1,), (1,)), ((), ())),
            preferred_element_type=jnp.float32,
        )
    column = lax.broadcasted_iota(jnp.int32, gram.shape, 1)
    sign = jnp.where((column // chunk) % 2 == 0, 1.0, -1.0)
    shifted = gram * (1.0 / full_width) + 1.0
    signed = shifted * shifted * sign
    proof[...] = jnp.sum(signed * shifted, axis=1, keepdims=True) * wit_scale
    weight[...] = (3.0 * signed).astype(jnp.bfloat16)
    for step, part in enumerate(parts):

        @pl.when(pl.program_id(0) == step)
        def _(part=part):
            gradient_part(grad_scale, weight[...], met, slots - 1, part)


def gradient_part(grad_scale, weight, met, slot, out):
    part = jnp.dot(weight, met[slot], preferred_element_type=jnp.float32)
    out[...] = (part * grad_scale).astype(out.dtype)


def rest_kernel(grad_scale, weight, met, *outs):
    for slot, out in enumerate(outs):
        gradient_part(grad_scale, weight[...], met, slot, out)


def total_kernel(grad_scale, slot, weight, met, got, out):
    part = jnp.dot(weight[...], met[slot], preferred_element_type=jnp.float32)
    out[...] = (part * grad_scale + got[...].astype(jnp.float32)).astype(out.dtype)


def final_kernel(mine, near, *refs):
    *crossed, out = refs
    for step, across in enumerate(crossed):

        @pl.when(pl.program_id(0) == step)
        def _(across=across):
            near_sum = mine[...] + near[...].astype(jnp.float32)
            out[...] = near_sum + across[...].astype(jnp.float32)


def untouched(shape, dtype):
    return pl.pallas_call(
        lambda out: None,
        out_specs=pl.BlockSpec(memory_space=pl.ANY),
        out_shape=jax.ShapeDtypeStruct(shape, dtype),
    )()


def on_device(generated, reference_set, partners):
    block_rows, feat_width = generated.shape
    groups = lax.axis_size("grp")
    full_width = feat_width * groups
    rounds_count = partners.shape[0]
    share = block_rows // groups
    wit_scale = (full_width / (rounds_count * block_rows)) ** 0.5
    grad_scale = 1.0 / (rounds_count * block_rows) ** 0.5
    here = lax.axis_index("grp")

    def chunk_for(member):
        return jnp.concatenate(
            [
                lax.dynamic_slice_in_dim(x, member * share, share)
                for x in (generated, reference_set)
            ]
        )

    pieces = [chunk_for(here)]
    for distance in range(1, groups):
        pieces.append(grp_swap(chunk_for(here ^ distance), distance))
    late = far_swap(jnp.stack(pieces[:1:-1]))
    early = far_swap(jnp.stack(pieces[1::-1]))
    own_rows = jnp.stack(pieces)
    masks = [partners[r, 0] for r in range(rounds_count)]
    far_bits = [(m >> 1) & 1 for m in masks]
    swapped = far_bits[0] > far_bits[1]
    masks = [
        jnp.where(swapped, masks[1], masks[0]),
        jnp.where(swapped, masks[0], masks[1]),
    ]
    near_count = rounds_count - far_bits[0] - far_bits[1]
    met = untouched((groups, rounds_count * 2 * share, feat_width), generated.dtype)
    own_rows, generated, masks, near_count, met = lax.optimization_barrier(
        (own_rows, generated, masks, near_count, met)
    )
    left = [generated] + [grp_swap(generated, d) for d in range(1, groups)]

    def put(met, got, index):
        return lax.dynamic_update_slice(met, got, (0, index * 2 * share, 0))

    def meet(rows):
        def body(index, carry):
            met, mask, later = carry
            got = plane_hop(rows, mask >> 2)
            met = lax.cond(
                (mask & CORE) > 0,
                lambda m, g, i: put(m, blk_swap(g, CORE), i),
                put,
                met,
                got,
                index,
            )
            return met, later, later

        return body

    carry = (met, *masks)
    carry = lax.fori_loop(0, near_count, meet(own_rows), carry)
    carry, late, early = lax.optimization_barrier((carry, late, early))
    far_rows = jnp.concatenate([late, early])
    met, _, _ = lax.fori_loop(near_count, rounds_count, meet(far_rows), carry)

    def tiled(width):
        return pl.BlockSpec((TILE, width), lambda i: (i, 0))

    def shaped(width, dtype):
        return jax.ShapeDtypeStruct((block_rows, width), dtype)

    once = pl.BlockSpec((TILE, feat_width), lambda i: (0, 0))
    whole = pl.BlockSpec(met.shape, lambda i: (0, 0, 0))
    params = pltpu.CompilerParams(vmem_limit_bytes=40 * 2**20)
    columns = met.shape[1]
    proof, weight, *across_parts = pl.pallas_call(
        lambda *refs: weight_kernel(full_width, grad_scale, wit_scale, share, *refs),
        grid=(block_rows // TILE,),
        in_specs=[tiled(feat_width)] * groups + [whole],
        out_specs=[tiled(1), tiled(columns)] + [once] * 2,
        out_shape=[shaped(1, jnp.float32), shaped(columns, jnp.bfloat16)]
        + [jax.ShapeDtypeStruct((TILE, feat_width), jnp.bfloat16)] * 2,
        compiler_params=params,
    )(*left, met)
    halves = [grp_swap(part, 1) for part in across_parts]
    mine, near_part = pl.pallas_call(
        lambda *refs: rest_kernel(grad_scale, *refs),
        grid=(block_rows // TILE,),
        in_specs=[tiled(columns), whole],
        out_specs=[tiled(feat_width)] * 2,
        out_shape=[shaped(feat_width, jnp.float32), shaped(feat_width, jnp.bfloat16)],
        compiler_params=params,
    )(weight, met)
    crossed = []
    for step, got in enumerate(halves):
        total = pl.pallas_call(
            lambda *refs: total_kernel(grad_scale, 2, *refs),
            grid=(1,),
            in_specs=[
                pl.BlockSpec((TILE, columns), lambda i, step=step: (step, 0)),
                whole,
                once,
            ],
            out_specs=once,
            out_shape=jax.ShapeDtypeStruct((TILE, feat_width), jnp.bfloat16),
            compiler_params=params,
        )(weight, met, got)
        crossed.append(grp_swap(total, 2))
    near_part, proof, _ = lax.optimization_barrier((near_part, proof, total))
    grads = pl.pallas_call(
        final_kernel,
        grid=(block_rows // TILE,),
        in_specs=[tiled(feat_width)] * 2 + [once] * len(crossed),
        out_specs=tiled(feat_width),
        out_shape=shaped(feat_width, jnp.float32),
        compiler_params=params,
    )(mine, grp_swap(near_part, 1), *crossed)
    proofs = jnp.broadcast_to(proof.reshape(1, block_rows), (groups, block_rows))
    proof = jnp.sum(lax.all_to_all(proofs, "grp", 0, 0), axis=0)
    return (proof, grads)


def solution(mesh):
    return jax.shard_map(
        on_device,
        mesh=mesh,
        in_specs=(P("blk", "grp"), P("blk", "grp"), P()),
        out_specs=(P("blk"), P("blk", "grp")),
        check_vma=False,
    )
```

```python
import jax
import jax.numpy as jnp
from jax import lax
from jax.experimental import pallas as pl
from jax.experimental.pallas import tpu as pltpu
from jax.sharding import PartitionSpec as P

TILE = 320
CORE, FAR = 1, 2


def grp_swap(value, distance):
    size = lax.axis_size("grp")
    return lax.ppermute(value, "grp", [(k, k ^ distance) for k in range(size)])


def blk_swap(value, mask):
    blocks = lax.axis_size("blk")
    return lax.ppermute(value, "blk", [(b, b ^ mask) for b in range(blocks)])


def far_swap(value):
    blocks, groups = lax.axis_size("blk"), lax.axis_size("grp")
    pairs = [
        (b * groups + k, (b ^ FAR) * groups + groups - 1 - k)
        for b in range(blocks)
        for k in range(groups)
    ]
    return lax.ppermute(value, ("blk", "grp"), pairs)


def plane_hop(value, step):
    stride = 2 * FAR
    masks = range(stride, lax.axis_size("blk"), stride)
    branches = [lambda v, m=m: blk_swap(v, m) for m in masks]
    return lax.switch(step, [lambda v: v] + branches, value)


def weight_kernel(full_width, grad_scale, wit_scale, chunk, *refs):
    slots = len(refs) - 5
    left, (met, proof, weight, *parts) = refs[:slots], refs[slots:]
    gram = jnp.zeros(weight.shape, jnp.float32)
    for slot in range(slots):
        gram += lax.dot_general(
            left[slot][...],
            met[slot],
            (((1,), (1,)), ((), ())),
            preferred_element_type=jnp.float32,
        )
    column = lax.broadcasted_iota(jnp.int32, gram.shape, 1)
    sign = jnp.where((column // chunk) % 2 == 0, 1.0, -1.0)
    shifted = gram * (1.0 / full_width) + 1.0
    signed = shifted * shifted * sign
    proof[...] = jnp.sum(signed * shifted, axis=1, keepdims=True) * wit_scale
    weight[...] = (3.0 * signed).astype(jnp.bfloat16)
    for step, part in enumerate(parts):

        @pl.when(pl.program_id(0) == step)
        def _(part=part):
            gradient_part(grad_scale, weight[...], met, slots - 1, part)


def gradient_part(grad_scale, weight, met, slot, out):
    part = jnp.dot(weight, met[slot], preferred_element_type=jnp.float32)
    out[...] = (part * grad_scale).astype(out.dtype)


def rest_kernel(grad_scale, weight, met, *outs):
    for slot, out in enumerate(outs):
        gradient_part(grad_scale, weight[...], met, slot, out)


def total_kernel(grad_scale, slot, weight, met, got, out):
    part = jnp.dot(weight[...], met[slot], preferred_element_type=jnp.float32)
    out[...] = (part * grad_scale + got[...].astype(jnp.float32)).astype(out.dtype)


def final_kernel(mine, near, *refs):
    *crossed, out = refs
    for step, across in enumerate(crossed):

        @pl.when(pl.program_id(0) == step)
        def _(across=across):
            near_sum = mine[...] + near[...].astype(jnp.float32)
            out[...] = near_sum + across[...].astype(jnp.float32)


def untouched(shape, dtype):
    return pl.pallas_call(
        lambda out: None,
        out_specs=pl.BlockSpec(memory_space=pl.ANY),
        out_shape=jax.ShapeDtypeStruct(shape, dtype),
    )()


def on_device(generated, reference_set, partners):
    block_rows, feat_width = generated.shape
    groups = lax.axis_size("grp")
    full_width = feat_width * groups
    rounds_count = partners.shape[0]
    share = block_rows // groups
    wit_scale = (full_width / (rounds_count * block_rows)) ** 0.5
    grad_scale = 1.0 / (rounds_count * block_rows) ** 0.5
    here = lax.axis_index("grp")

    def chunk_for(member):
        return jnp.concatenate(
            [
                lax.dynamic_slice_in_dim(x, member * share, share)
                for x in (generated, reference_set)
            ]
        )

    pieces = [chunk_for(here)]
    for distance in range(1, groups):
        pieces.append(grp_swap(chunk_for(here ^ distance), distance))
    masks = [partners[r, 0] for r in range(rounds_count)]
    far_bits = [(m >> 1) & 1 for m in masks]
    swapped = far_bits[0] > far_bits[1]
    masks = [
        jnp.where(swapped, masks[1], masks[0]),
        jnp.where(swapped, masks[0], masks[1]),
    ]
    near_count = rounds_count - far_bits[0] - far_bits[1]
    met = untouched((groups, rounds_count * 2 * share, feat_width), generated.dtype)
    pieces[1], masks, near_count, met = lax.optimization_barrier(
        (pieces[1], masks, near_count, met)
    )
    late = far_swap(jnp.stack(pieces[:1:-1]))
    early = far_swap(jnp.stack(pieces[1::-1]))
    own_rows = jnp.stack(pieces)
    own_rows, generated = lax.optimization_barrier((own_rows, generated))
    others = [grp_swap(generated, d) for d in range(2, groups)]

    def put(met, got, index):
        return lax.dynamic_update_slice(met, got, (0, index * 2 * share, 0))

    def meet(rows):
        def body(index, carry):
            met, mask, later = carry
            got = plane_hop(rows, mask >> 2)
            met = lax.cond(
                (mask & CORE) > 0,
                lambda m, g, i: put(m, blk_swap(g, CORE), i),
                put,
                met,
                got,
                index,
            )
            return met, later, later

        return body

    carry = (met, *masks)
    carry = lax.fori_loop(0, near_count, meet(own_rows), carry)
    carry, late, early, generated = lax.optimization_barrier(
        (carry, late, early, generated)
    )
    left = [generated, grp_swap(generated, 1)] + others
    far_rows = jnp.concatenate([late, early])
    met, _, _ = lax.fori_loop(near_count, rounds_count, meet(far_rows), carry)

    def tiled(width):
        return pl.BlockSpec((TILE, width), lambda i: (i, 0))

    def shaped(width, dtype):
        return jax.ShapeDtypeStruct((block_rows, width), dtype)

    once = pl.BlockSpec((TILE, feat_width), lambda i: (0, 0))
    whole = pl.BlockSpec(met.shape, lambda i: (0, 0, 0))
    params = pltpu.CompilerParams(vmem_limit_bytes=40 * 2**20)
    columns = met.shape[1]
    proof, weight, *across_parts = pl.pallas_call(
        lambda *refs: weight_kernel(full_width, grad_scale, wit_scale, share, *refs),
        grid=(block_rows // TILE,),
        in_specs=[tiled(feat_width)] * groups + [whole],
        out_specs=[tiled(1), tiled(columns)] + [once] * 2,
        out_shape=[shaped(1, jnp.float32), shaped(columns, jnp.bfloat16)]
        + [jax.ShapeDtypeStruct((TILE, feat_width), jnp.bfloat16)] * 2,
        compiler_params=params,
    )(*left, met)
    halves = [grp_swap(part, 1) for part in across_parts]
    mine, near_part = pl.pallas_call(
        lambda *refs: rest_kernel(grad_scale, *refs),
        grid=(block_rows // TILE,),
        in_specs=[tiled(columns), whole],
        out_specs=[tiled(feat_width)] * 2,
        out_shape=[shaped(feat_width, jnp.float32), shaped(feat_width, jnp.bfloat16)],
        compiler_params=params,
    )(weight, met)
    crossed = []
    for step, got in enumerate(halves):
        total = pl.pallas_call(
            lambda *refs: total_kernel(grad_scale, 2, *refs),
            grid=(1,),
            in_specs=[
                pl.BlockSpec((TILE, columns), lambda i, step=step: (step, 0)),
                whole,
                once,
            ],
            out_specs=once,
            out_shape=jax.ShapeDtypeStruct((TILE, feat_width), jnp.bfloat16),
            compiler_params=params,
        )(weight, met, got)
        crossed.append(grp_swap(total, 2))
    near_part, proof, _ = lax.optimization_barrier((near_part, proof, total))
    grads = pl.pallas_call(
        final_kernel,
        grid=(block_rows // TILE,),
        in_specs=[tiled(feat_width)] * 2 + [once] * len(crossed),
        out_specs=tiled(feat_width),
        out_shape=shaped(feat_width, jnp.float32),
        compiler_params=params,
    )(mine, grp_swap(near_part, 1), *crossed)
    proofs = jnp.broadcast_to(proof.reshape(1, block_rows), (groups, block_rows))
    proof = jnp.sum(lax.all_to_all(proofs, "grp", 0, 0), axis=0)
    return (proof, grads)


def solution(mesh):
    return jax.shard_map(
        on_device,
        mesh=mesh,
        in_specs=(P("blk", "grp"), P("blk", "grp"), P()),
        out_specs=(P("blk"), P("blk", "grp")),
        check_vma=False,
    )
```
